32 devices in a mesh: grp: 2 (over x), exp: 16 (over z, y, core).
Axes of the slice: x: 2, y: 2, z: 4, core: 2. Of those that a mesh axis runs over, the one named last changes fastest.
Arguments:
- tokens: bfloat16 [128, 6144], P(('grp', 'exp')), parts along dimension 0, may hold values from -6 to 6
- expert_ids: int32 [128, 2], P(('grp', 'exp')), parts along dimension 0, may hold values from 0 to 3, all different within a row; in each aligned block of 4 rows (0 to 3, 4 to 7, ...) at most 3 rows name the same one
- router_weight: bfloat16 [6144, 4], replicated, may hold values from -0.15625 to 0.15625
- gate_weight: bfloat16 [16, 6144, 2048], P('exp'), may hold values from -0.078125 to 0.078125
- up_weight: bfloat16 [16, 6144, 2048], P('exp'), may hold values from -0.078125 to 0.078125
- down_weight: bfloat16 [16, 2048, 6144], P('exp'), may hold values from -0.0625 to 0.0625
Outputs:
- mixed: bfloat16 [128, 6144], P(('grp', 'exp')), parts along dimension 0
The draws below stay inside these ranges and needn't reach their ends.
There are 2 independent parts, one for each index of `grp`. The reference program is written for one: setup_inputs(seed, part) draws one part's arguments, and reference() takes and returns one part's arrays. A program takes and returns all parts, laid end to end along the dimension named above; an argument that names none is the same for every part. Nothing has to cross between parts.
Inputs may be any that keep to these rules, and one draw needn't show every extreme that they name: `expert_ids`: the two ids of a token differ. Among the 4 tokens of one device (rows j * 4 to (j + 1) * 4 - 1), no expert is named more than 3 times, and in every draw some device names some expert exactly 3 times.
All inputs are finite; a program needn't handle non-finite values.
Results may differ from the reference program's by a relative error of at most 0.0059.
Values may be sent and summed in bfloat16 or wider, within the bound.
A program may use at most 192 MiB of HBM per device.

```python
import math
import jax
import jax.numpy as jnp
import numpy as np

D = 6144
FF = 8192
EXPERTS = 4
TOP = 2
TOK = 4
CAP = 3
GROUP = 4
HSLICE = 2048
TOKENS = 64


def level_of(stream_key, shape, shards, least, top_value):
    gain = 1.0
    for axis_at, parts in shards:
        draws = jax.random.uniform(jax.random.fold_in(jax.random.fold_in(stream_key, 6), axis_at), (parts,), jnp.float32, least / len(shards), top_value / len(shards))
        gain = gain * jnp.repeat(jnp.exp(draws), shape[axis_at] // parts).reshape((-1,) + (1,) * (len(shape) - 1 - axis_at))
    return gain


def shared_out(stream_key, own, number, rows, amount, top, bound, skew):
    order = jax.random.permutation(stream_key, amount)
    heavy_load, common = load_shares(amount, rows * top, bound, skew, True), load_shares(amount, rows * top, bound, skew, False)
    places = jnp.arange(amount)

    def named(lengths, turn):
        used = int((lengths > 0).sum())
        fixed = max(1, used // 4)
        moved = fixed + (places - fixed + turn * (used - fixed)) % max(1, amount - fixed)
        return jnp.zeros((amount,), jnp.int32).at[order[jnp.where(places < fixed, places, moved)]].set(jnp.asarray(lengths, jnp.int32))

    lengths = jnp.where(number % 4 == 0, named(heavy_load, number // 4), named(common, number - number // 4 - 1))
    mixed = jax.random.permutation(jax.random.fold_in(own, 3), amount)
    source_of, receiver = mixed[0:amount // 2 * 2:2], mixed[1:amount // 2 * 2:2]
    margin = jnp.minimum(lengths[source_of] - 1, bound - lengths[receiver]) // 2
    margin = jnp.where((source_of == order[0]) | (receiver == order[0]) | (lengths[receiver] == 0), 0, jnp.maximum(margin, 0))
    moved = jax.random.randint(jax.random.fold_in(own, 4), (amount // 2,), 0, 1 << 20) % (margin + 1)
    lengths = lengths.at[source_of].add(-moved).at[receiver].add(moved)
    labels = jnp.searchsorted(jnp.cumsum(lengths), jnp.arange(rows * top), side="right").astype(jnp.int32)
    listing = labels.reshape(top, rows).T
    listing = listing[jax.random.permutation(jax.random.fold_in(own, 1), rows)]
    turn = jax.random.randint(jax.random.fold_in(own, 2), (rows, 1), 0, top)
    return jnp.take_along_axis(listing, (jnp.arange(top)[None, :] + turn) % top, axis=1)


def load_shares(number_of, total, bound, lean, full):
    portions = [(1 << 20) // math.isqrt(standing ** lean) + 1 for standing in range(1, number_of + 1)]
    largest = bound if full else min(bound, max(-(-total // number_of), total * portions[0] // sum(portions)))
    least = 1 if total - largest >= number_of - 1 else 0
    counts, rest = [largest] + [least] * (number_of - 1), total - largest - least * (number_of - 1)
    while rest > 0:
        candidates = [i for i in range(1, number_of) if counts[i] < largest] or [i for i in range(1, number_of) if counts[i] < bound]
        mass, budget = sum([portions[i] for i in candidates]), rest
        for i in candidates:
            more = min(bound - counts[i], max(1, budget * portions[i] // mass), rest)
            counts[i] = counts[i] + more
            rest = rest - more
    return np.array(counts)


def centred(rng, extent, scale, bound, split=(), kind=jnp.bfloat16):
    entries = jax.random.normal(rng, extent, jnp.float32) * scale
    if len(split) > 0:
        entries = level_of(rng, extent, split, -0.22, 0.18) * entries
    return jnp.clip(entries, min=-bound, max=bound).astype(kind)


def setup_inputs(seed: int = 0, part: int = 0) -> dict:
    splits = jax.random.split(jax.random.key(seed), 7)
    own_keys = jax.random.split(jax.random.fold_in(splits[6], part), 7)
    tokens = centred(own_keys[0], (TOKENS, D), 1.0, 6.0, ((0, 16),))
    expert_ids_keys = jax.random.split(jax.random.fold_in(own_keys[1], 1), TOKENS // TOK)
    expert_ids_turns = jax.random.permutation(jax.random.fold_in(own_keys[1], 3), TOKENS // TOK)
    expert_ids = jax.vmap(lambda own, number: shared_out(jax.random.fold_in(own_keys[1], 2), own, number, TOK, EXPERTS, 2, CAP, 2))(expert_ids_keys, expert_ids_turns).reshape((TOKENS, TOP))
    router_weight = centred(splits[2], (D, EXPERTS), (D // 4) ** -0.5, 0.15625)
    gate_weight = centred(splits[3], (GROUP * EXPERTS, D, HSLICE), D ** -0.5, 0.078125, ((0, 16),))
    up_weight = centred(splits[4], (GROUP * EXPERTS, D, HSLICE), D ** -0.5, 0.078125, ((0, 16),))
    down_weight = centred(splits[5], (GROUP * EXPERTS, HSLICE, D), FF ** -0.5, 0.0625, ((0, 16),))
    return dict(tokens=tokens, expert_ids=expert_ids, router_weight=router_weight, gate_weight=gate_weight, up_weight=up_weight, down_weight=down_weight)


def reference(tokens, expert_ids, router_weight, gate_weight, up_weight, down_weight):
    logits = jnp.dot(tokens, router_weight, preferred_element_type=jnp.float32)
    expert_iota = jnp.arange(EXPERTS, dtype=jnp.int32)
    pick_first = expert_ids[:, 0:1] == expert_iota[None, :]
    pick_second = expert_ids[:, 1:2] == expert_iota[None, :]
    logit_first = jnp.sum(jnp.where(pick_first, logits, 0.0), axis=1)
    logit_second = jnp.sum(jnp.where(pick_second, logits, 0.0), axis=1)
    weight_first = 1.0 / (1.0 + jnp.exp(logit_second - logit_first))
    weight_second = 1.0 / (1.0 + jnp.exp(logit_first - logit_second))
    weight_table = jnp.where(pick_first, weight_first[:, None], 0.0) + jnp.where(pick_second, weight_second[:, None], 0.0)
    gate_blocks = gate_weight.reshape(GROUP, EXPERTS, D, HSLICE)
    up_blocks = up_weight.reshape(GROUP, EXPERTS, D, HSLICE)
    down_blocks = down_weight.reshape(GROUP, EXPERTS, HSLICE, D)
    mixed = jnp.zeros((TOKENS, D), jnp.float32)
    for expert_index in range(EXPERTS):
        gate_full = jnp.transpose(gate_blocks[:, expert_index], (1, 0, 2)).reshape(D, FF)
        up_full = jnp.transpose(up_blocks[:, expert_index], (1, 0, 2)).reshape(D, FF)
        down_full = down_blocks[:, expert_index].reshape(FF, D)
        gate_part = jnp.dot(tokens, gate_full, preferred_element_type=jnp.float32)
        up_part = jnp.dot(tokens, up_full, preferred_element_type=jnp.float32)
        hidden = (jax.nn.silu(gate_part) * up_part).astype(jnp.bfloat16)
        expert_out = jnp.dot(hidden, down_full, preferred_element_type=jnp.float32).astype(jnp.bfloat16)
        mixed = mixed + weight_table[:, expert_index:expert_index + 1] * expert_out.astype(jnp.float32)
    return mixed.astype(jnp.bfloat16)
```

```python
import functools

import jax
import jax.numpy as jnp
from jax import lax
from jax.experimental import pallas as pl
from jax.experimental.pallas import tpu as pltpu
from jax.sharding import PartitionSpec as P

MESH = pl.DeviceIdType.MESH
F32 = jnp.float32
BF16 = jnp.bfloat16
LANES = 128
PLANE = 4
ROWS = 16


def divisor_at_most(total, most):
    return max(size for size in range(LANES, most + 1, LANES) if total % size == 0)


class Plan:
    def __init__(self, devices, tok, width, hidden):
        self.devices, self.tok, self.width, self.hidden = devices, tok, width, hidden
        self.slots = devices // PLANE
        self.pieces = ROWS // tok
        self.piece = width // self.pieces
        self.ext = self.piece + LANES
        self.tokens = devices * tok
        self.half = self.tokens // 2
        self.quarter = self.tokens // 4
        self.up_rows = divisor_at_most(width, min(2048, 2 * hidden))
        self.up_cols = divisor_at_most(hidden, 512)
        self.k_steps = width // self.up_rows
        self.n_steps = hidden // self.up_cols
        self.per_n = 2 * self.k_steps
        self.first = self.per_n * self.n_steps
        self.down_cols = divisor_at_most(width, 512)
        self.downs = width // self.down_cols
        self.buffers = max(self.first, self.downs)
        self.group = 2
        self.groups = self.downs // self.group
        self.cols = self.group * self.down_cols
        self.part = self.cols // self.pieces


def kernel(
    p, experts, tok_ref, ids_ref, router_ref, gate_ref, up_ref, down_ref, out_ref,
    wbuf, x, stage, lhs, hid, table, keep, a_send, a_recv, b_own, b_send, b_recv,
    z_full, z_stage, z_send, z_recv, out_f32,
    wsem, gs_z, gr_z, gs_y, gr_y, gs_c, gr_c, sa, ra, sb, rb, sc, rc,
):
    grp = lax.axis_index("grp")
    me = lax.axis_index("exp")
    slot, e = me // PLANE, me % PLANE
    core, ypos = e % 2, e // 2
    core_peer = slot * PLANE + ypos * 2 + (1 - core)
    y_peer = slot * PLANE + (1 - ypos) * 2 + core

    def first_copy(n, m):
        k, ref = m // 2, (gate_ref, up_ref)[m % 2]
        at = n * p.per_n + m
        cols = pl.ds(pl.multiple_of(n * p.up_cols, p.up_cols), p.up_cols)
        return pltpu.make_async_copy(
            ref.at[0, pl.ds(k * p.up_rows, p.up_rows), cols],
            wbuf.at[at, pl.ds(0, p.up_rows), pl.ds(0, p.up_cols)],
            wsem.at[at],
        )

    def down_copy(j):
        cols = pl.ds(pl.multiple_of(j * p.down_cols, p.down_cols), p.down_cols)
        return pltpu.make_async_copy(
            down_ref.at[0, :, cols],
            wbuf.at[j, pl.ds(0, p.hidden), pl.ds(0, p.down_cols)],
            wsem.at[j],
        )

    def remote(src, dst, send, recv, device):
        return pltpu.make_async_remote_copy(
            src_ref=src, dst_ref=dst, send_sem=send, recv_sem=recv,
            device_id=(grp, device), device_id_type=MESH,
        )

    barrier = pltpu.get_barrier_semaphore()
    z_peers = [lax.rem(slot + d, p.slots) * PLANE + e for d in range(1, p.slots)]
    for peer in z_peers + [y_peer, core_peer]:
        pl.semaphore_signal(barrier, inc=1, device_id=(grp, peer), device_id_type=MESH)

    for m in range(p.per_n):
        first_copy(0, m).start()

    lane = lax.broadcasted_iota(jnp.int32, (p.tok, LANES), 1)
    line = lax.broadcasted_iota(jnp.int32, (p.tok, LANES), 0)
    ids = jnp.zeros((p.tok, LANES), jnp.int32)
    for t in range(p.tok):
        named = jnp.where(lane < LANES // 2, ids_ref[0, t], ids_ref[1, t])
        ids = jnp.where(line == t, named, ids)
    for c in range(p.pieces):
        rows = pl.ds(c * p.tok, p.tok)
        stage[rows, pl.ds(0, p.piece)] = tok_ref[:, pl.ds(c * p.piece, p.piece)].astype(F32)
        stage[rows, pl.ds(p.piece, LANES)] = ids.astype(F32)
    x[me] = stage[...].astype(BF16)

    pl.semaphore_wait(barrier, p.slots + 1)

    started = []

    def send(copy):
        copy.start()
        started.append(copy)

    for d in range(1, p.slots):
        send(remote(x.at[me], x.at[me], gs_z.at[d], gr_z.at[d], z_peers[d - 1]))
    send(remote(x.at[me], x.at[me], gs_y.at[0], gr_y.at[0], y_peer))
    send(remote(x.at[me], x.at[me], gs_c.at[0], gr_c.at[0], core_peer))

    for n in range(1, p.n_steps):
        for m in range(p.per_n):
            first_copy(n, m).start()
    for j in range(p.first, p.downs):
        down_copy(j).start()

    for d in range(1, p.slots):
        block = lax.rem(slot + p.slots - d, p.slots) * PLANE + e
        remote(x.at[block], x.at[block], gs_z.at[d], gr_z.at[d], me ^ 1).wait_recv()
        send(remote(x.at[block], x.at[block], gs_y.at[d], gr_y.at[d], y_peer))
        send(remote(x.at[block], x.at[block], gs_c.at[d], gr_c.at[d], core_peer))
    for d in range(p.slots):
        block = lax.rem(slot + p.slots - d, p.slots) * PLANE + (1 - ypos) * 2 + core
        remote(x.at[block], x.at[block], gs_y.at[d], gr_y.at[d], y_peer).wait_recv()
        at = p.slots + d
        send(remote(x.at[block], x.at[block], gs_c.at[at], gr_c.at[at], core_peer))
    for d in range(p.slots):
        for side in range(2):
            ye = ypos if side == 0 else 1 - ypos
            block = lax.rem(slot + p.slots - d, p.slots) * PLANE + ye * 2 + (1 - core)
            at = side * p.slots + d
            remote(x.at[block], x.at[block], gs_c.at[at], gr_c.at[at], core_peer).wait_recv()

    blocks = p.quarter
    row_in = lax.broadcasted_iota(jnp.int32, (p.quarter, p.devices * ROWS), 0)
    col_in = lax.broadcasted_iota(jnp.int32, (p.quarter, p.devices * ROWS), 1)
    for q in range(PLANE):
        dest_core, dest_y = q // 2, q % 2
        device = (row_in // p.tok) * PLANE + dest_y * 2 + dest_core
        for c in range(p.pieces):
            pick = (col_in == device * ROWS + c * p.tok + row_in % p.tok)
            pick = jnp.where(pick, 1.0, 0.0).astype(BF16)
            flat = x[...].reshape(p.devices * ROWS, p.ext)
            got = jnp.dot(pick, flat, preferred_element_type=F32)
            lhs[pl.ds(q * p.quarter, p.quarter), pl.ds(c * p.piece, p.piece)] = (
                got[:, : p.piece].astype(BF16)
            )
            if c == 0:
                table[pl.ds(q * p.quarter, p.quarter), :] = got[:, p.piece:]

    @pl.loop(0, p.n_steps)
    def _(n):
        sums = [None, None]
        for m in range(p.per_n):
            first_copy(n, m).wait()
            k = m // 2
            part = jnp.dot(
                lhs[:, pl.ds(k * p.up_rows, p.up_rows)],
                wbuf[n * p.per_n + m, pl.ds(0, p.up_rows), pl.ds(0, p.up_cols)],
                preferred_element_type=F32,
            )
            sums[m % 2] = part if k == 0 else sums[m % 2] + part
        g, u = sums
        cols = pl.ds(pl.multiple_of(n * p.up_cols, p.up_cols), p.up_cols)
        hid[:, cols] = (g / (1.0 + jnp.exp(-g)) * u).astype(BF16)
        for m in range(p.per_n):
            @pl.when(n * p.per_n + m < p.downs)
            def _():
                down_copy(n * p.per_n + m).start()

    logits = lax.dot_general(
        lhs[...], router_ref[...], (((1,), (1,)), ((), ())), preferred_element_type=F32
    )
    ids = table[...]
    id_a, id_b = ids[:, 0:1], ids[:, LANES // 2 : LANES // 2 + 1]
    iota = lax.broadcasted_iota(jnp.int32, logits.shape, 1).astype(F32)
    logit_a = jnp.sum(jnp.where(iota == id_a, logits, 0.0), axis=1, keepdims=True)
    logit_b = jnp.sum(jnp.where(iota == id_b, logits, 0.0), axis=1, keepdims=True)
    mine = e.astype(F32)
    weight = jnp.where(id_a == mine, 1.0 / (1.0 + jnp.exp(logit_b - logit_a)), 0.0)
    weight += jnp.where(id_b == mine, 1.0 / (1.0 + jnp.exp(logit_a - logit_b)), 0.0)
    table[...] = jnp.broadcast_to(weight, table.shape)

    def copy_a(g):
        return remote(a_send.at[g], a_recv.at[g], sa.at[g], ra.at[g], core_peer)

    def copy_b(g):
        return remote(b_send.at[g], b_recv.at[g], sb.at[g], rb.at[g], y_peer)

    def copy_c(g, d):
        dest = lax.rem(slot + d, p.slots)
        return remote(
            z_send.at[g, dest], z_recv.at[g, d], sc.at[g, d], rc.at[g, d],
            dest * PLANE + e,
        )

    def compute(g):
        for i in range(p.group):
            j = g * p.group + i
            down_copy(j).wait()
            part = jnp.dot(
                hid[...], wbuf[j, pl.ds(0, p.hidden), pl.ds(0, p.down_cols)],
                preferred_element_type=F32,
            )
            part = part * table[:, 0:1]
            cols = pl.ds(i * p.down_cols, p.down_cols)
            low, high = part[: p.half], part[p.half :]
            is_low = core == 0
            keep[g, :, cols] = jnp.where(is_low, low, high)
            a_send[g, :, cols] = jnp.where(is_low, high, low).astype(BF16)
        copy_a(g).start()

    def second(g):
        copy_a(g).wait()
        total = keep[g] + a_recv[g].astype(F32)
        low, high = total[: p.quarter], total[p.quarter :]
        b_own[g] = jnp.where(ypos == 0, low, high)
        b_send[g] = jnp.where(ypos == 0, high, low).astype(BF16)
        copy_b(g).start()

    def third(g):
        copy_b(g).wait()
        z_full[...] = b_own[g] + b_recv[g].astype(F32)
        for s in range(p.slots):
            for c in range(p.pieces):
                z_stage[s, pl.ds(c * p.tok, p.tok), :] = z_full[
                    pl.ds(s * p.tok, p.tok), pl.ds(c * p.part, p.part)
                ]
        z_send[g] = z_stage[...].astype(BF16)
        b_own[g, pl.ds(0, ROWS), pl.ds(0, p.part)] = z_stage[slot]
        for d in range(1, p.slots):
            copy_c(g, d).start()

    @pl.loop(0, p.groups + 2)
    def _(it):
        @pl.when(it < p.groups)
        def _():
            compute(it)

        @pl.when((it >= 1) & (it < p.groups + 1))
        def _():
            second(it - 1)

        @pl.when(it >= 2)
        def _():
            third(it - 2)

    @pl.loop(0, p.groups)
    def _(g):
        total = b_own[g, pl.ds(0, ROWS), pl.ds(0, p.part)]
        for d in range(1, p.slots):
            copy_c(g, d).wait()
            total = total + z_recv[g, d].astype(F32)
        out_f32[...] = total
        for c in range(p.pieces):
            at = pl.multiple_of(g * p.cols + c * p.part, p.part)
            out_ref[:, pl.ds(at, p.part)] = out_f32[pl.ds(c * p.tok, p.tok), :].astype(BF16)

    for copy in started:
        copy.wait_send()


def shards(devices, tokens, expert_ids, router_weight, gate_weight, up_weight, down_weight):
    tok, width = tokens.shape
    experts = router_weight.shape[1]
    hidden = gate_weight.shape[2]
    p = Plan(devices, tok, width, hidden)
    vmem = pl.BlockSpec(memory_space=pltpu.VMEM)
    hbm = pl.BlockSpec(memory_space=pl.ANY)
    dma = pltpu.SemaphoreType.DMA
    scratch = [
        pltpu.VMEM((p.buffers, max(p.up_rows, hidden), max(p.up_cols, p.down_cols)), BF16),
        pltpu.VMEM((devices, ROWS, p.ext), BF16),
        pltpu.VMEM((ROWS, p.ext), F32),
        pltpu.VMEM((p.tokens, width), BF16),
        pltpu.VMEM((p.tokens, hidden), BF16),
        pltpu.VMEM((p.tokens, LANES), F32),
        pltpu.VMEM((p.groups, p.half, p.cols), F32),
        pltpu.VMEM((p.groups, p.half, p.cols), BF16),
        pltpu.VMEM((p.groups, p.half, p.cols), BF16),
        pltpu.VMEM((p.groups, p.quarter, p.cols), F32),
        pltpu.VMEM((p.groups, p.quarter, p.cols), BF16),
        pltpu.VMEM((p.groups, p.quarter, p.cols), BF16),
        pltpu.VMEM((p.quarter, p.cols), F32),
        pltpu.VMEM((p.slots, ROWS, p.part), F32),
        pltpu.VMEM((p.groups, p.slots, ROWS, p.part), BF16),
        pltpu.VMEM((p.groups, p.slots, ROWS, p.part), BF16),
        pltpu.VMEM((ROWS, p.part), F32),
        dma((p.buffers,)),
        dma((p.slots,)), dma((p.slots,)), dma((p.slots,)), dma((p.slots,)),
        dma((2 * p.slots,)), dma((2 * p.slots,)),
        dma((p.groups,)), dma((p.groups,)), dma((p.groups,)), dma((p.groups,)),
        dma((p.groups, p.slots)), dma((p.groups, p.slots)),
    ]
    return pl.pallas_call(
        functools.partial(kernel, p, experts),
        out_shape=jax.ShapeDtypeStruct((tok, width), BF16),
        in_specs=[vmem, pl.BlockSpec(memory_space=pltpu.SMEM), vmem, hbm, hbm, hbm],
        out_specs=vmem,
        scratch_shapes=scratch,
        compiler_params=pltpu.CompilerParams(
            collective_id=0, has_side_effects=True, vmem_limit_bytes=60 * 2**20
        ),
        cost_estimate=pl.CostEstimate(
            flops=6 * p.tokens * width * hidden,
            bytes_accessed=6 * width * hidden,
            transcendentals=p.tokens * hidden,
        ),
        name="moe_decode",
    )(tokens, expert_ids.T, router_weight.T, gate_weight, up_weight, down_weight)


def solution(mesh):
    return jax.shard_map(
        functools.partial(shards, mesh.shape["exp"]),
        mesh=mesh,
        in_specs=(
            P(("grp", "exp"), None),
            P(("grp", "exp"), None),
            P(),
            P("exp", None, None),
            P("exp", None, None),
            P("exp", None, None),
        ),
        out_specs=P(("grp", "exp"), None),
        check_vma=False,
    )
```

```python
import functools

import jax
import jax.numpy as jnp
from jax import lax
from jax.experimental import pallas as pl
from jax.experimental.pallas import tpu as pltpu
from jax.sharding import PartitionSpec as P

MESH = pl.DeviceIdType.MESH
F32 = jnp.float32
BF16 = jnp.bfloat16
LANES = 128
PLANE = 4
SPLIT = 32
LAG = 2
ROWS = 16


def divisor_at_most(total, most):
    return max(size for size in range(LANES, most + 1, LANES) if total % size == 0)


class Plan:
    def __init__(self, devices, tok, width, hidden):
        self.devices, self.tok, self.width, self.hidden = devices, tok, width, hidden
        self.slots = devices // PLANE
        self.pieces = ROWS // tok
        self.piece = width // self.pieces
        self.ext = self.piece + LANES
        middle = self.ext // LANES // 2 * LANES
        self.spans = ((0, middle), (middle, self.ext - middle))
        self.tokens = devices * tok
        self.half = self.tokens // 2
        self.quarter = self.tokens // 4
        self.up_rows = divisor_at_most(width, min(2048, 2 * hidden))
        self.up_cols = divisor_at_most(hidden, 512)
        self.k_steps = width // self.up_rows
        self.n_steps = hidden // self.up_cols
        self.per_n = 2 * self.k_steps
        self.first = self.per_n * self.n_steps
        self.down_cols = divisor_at_most(width, 512)
        self.downs = width // self.down_cols
        self.buffers = max(self.first, self.downs)
        self.group = 2
        self.groups = self.downs // self.group
        self.cols = self.group * self.down_cols
        self.part = self.cols // self.pieces


def kernel(
    p, experts, tok_ref, ids_ref, router_ref, gate_ref, up_ref, down_ref, out_ref,
    wbuf, x, stage, lhs, hid, table, keep, a_send, a_recv, b_own, b_send, b_recv,
    z_full, z_stage, z_send, z_recv, out_f32,
    wsem, gs_z, gr_z, gs_y, gr_y, gs_c, gr_c, sa, ra, sb, rb, sc, rc,
):
    grp = lax.axis_index("grp")
    me = lax.axis_index("exp")
    slot, e = me // PLANE, me % PLANE
    core, ypos = e % 2, e // 2
    core_peer = slot * PLANE + ypos * 2 + (1 - core)
    y_peer = slot * PLANE + (1 - ypos) * 2 + core

    def first_copy(n, m):
        k, ref = m // 2, (gate_ref, up_ref)[m % 2]
        at = n * p.per_n + m
        cols = pl.ds(pl.multiple_of(n * p.up_cols, p.up_cols), p.up_cols)
        return pltpu.make_async_copy(
            ref.at[0, pl.ds(k * p.up_rows, p.up_rows), cols],
            wbuf.at[at, pl.ds(0, p.up_rows), pl.ds(0, p.up_cols)],
            wsem.at[at],
        )

    def down_copy(j):
        cols = pl.ds(pl.multiple_of(j * p.down_cols, p.down_cols), p.down_cols)
        return pltpu.make_async_copy(
            down_ref.at[0, :, cols],
            wbuf.at[j, pl.ds(0, p.hidden), pl.ds(0, p.down_cols)],
            wsem.at[j],
        )

    def remote(src, dst, send, recv, device):
        return pltpu.make_async_remote_copy(
            src_ref=src, dst_ref=dst, send_sem=send, recv_sem=recv,
            device_id=(grp, device), device_id_type=MESH,
        )

    barrier = pltpu.get_barrier_semaphore()
    z_peers = [lax.rem(slot + d, p.slots) * PLANE + e for d in range(1, p.slots)]
    for peer in z_peers + [y_peer, core_peer]:
        pl.semaphore_signal(barrier, inc=1, device_id=(grp, peer), device_id_type=MESH)

    for m in range(p.per_n):
        first_copy(0, m).start()

    lane = lax.broadcasted_iota(jnp.int32, (p.tok, LANES), 1)
    line = lax.broadcasted_iota(jnp.int32, (p.tok, LANES), 0)
    id_a = jnp.zeros((p.tok, LANES), jnp.int32)
    id_b = id_a
    for t in range(p.tok):
        id_a = jnp.where(line == t, ids_ref[0, t], id_a)
        id_b = jnp.where(line == t, ids_ref[1, t], id_b)
    own = tok_ref[...].astype(F32)
    logit_a = jnp.zeros((p.tok, LANES), F32)
    logit_b = logit_a
    for expert in range(experts):
        row = router_ref[pl.ds(expert, 1), :].astype(F32)
        logit = jnp.sum(own * row, axis=1, keepdims=True)
        logit_a = jnp.where(id_a == expert, logit, logit_a)
        logit_b = jnp.where(id_b == expert, logit, logit_b)
    named = lane % SPLIT
    weight = jnp.where(named == id_a, 1.0 / (1.0 + jnp.exp(logit_b - logit_a)), 0.0)
    weight += jnp.where(named == id_b, 1.0 / (1.0 + jnp.exp(logit_a - logit_b)), 0.0)
    high = weight.astype(BF16).astype(F32)
    middle = (weight - high).astype(BF16).astype(F32)
    terms = jnp.where(lane < SPLIT, high, jnp.where(lane < 2 * SPLIT, middle, weight - high - middle))
    terms = jnp.where(lane < 3 * SPLIT, terms, 0.0)
    for c in range(p.pieces):
        rows = pl.ds(c * p.tok, p.tok)
        stage[rows, pl.ds(0, p.piece)] = tok_ref[:, pl.ds(c * p.piece, p.piece)].astype(F32)
        stage[rows, pl.ds(p.piece, LANES)] = terms
    x[me] = stage[...].astype(BF16)

    pl.semaphore_wait(barrier, p.slots + 1)

    started = []

    def send(copy):
        copy.start()
        started.append(copy)

    def block_copy(block, h, send_sems, recv_sems, at, device):
        cols = pl.ds(*p.spans[h])
        ref = x.at[block, :, cols]
        return remote(ref, ref, send_sems.at[h, at], recv_sems.at[h, at], device)

    def z_block(d):
        return lax.rem(slot + p.slots - d, p.slots) * PLANE

    spans = range(len(p.spans))
    for h in spans:
        for d in range(1, p.slots):
            send(block_copy(me, h, gs_z, gr_z, d, z_peers[d - 1]))
        send(block_copy(me, h, gs_y, gr_y, 0, y_peer))
    for h in spans:
        send(block_copy(me, h, gs_c, gr_c, 0, core_peer))

    for n in range(1, p.n_steps):
        for m in range(p.per_n):
            first_copy(n, m).start()
    for j in range(p.first, p.downs):
        down_copy(j).start()

    for h in spans:
        for d in range(1, p.slots):
            block = z_block(d) + e
            block_copy(block, h, gs_z, gr_z, d, core_peer).wait_recv()
            send(block_copy(block, h, gs_y, gr_y, d, y_peer))
            send(block_copy(block, h, gs_c, gr_c, d, core_peer))
    for h in spans:
        for d in range(p.slots):
            block = z_block(d) + (1 - ypos) * 2 + core
            block_copy(block, h, gs_y, gr_y, d, y_peer).wait_recv()
            send(block_copy(block, h, gs_c, gr_c, p.slots + d, core_peer))
    for h in spans:
        for side in range(2):
            ye = ypos if side == 0 else 1 - ypos
            for d in range(p.slots):
                block = z_block(d) + ye * 2 + (1 - core)
                at = side * p.slots + d
                block_copy(block, h, gs_c, gr_c, at, core_peer).wait_recv()

    row_in = lax.broadcasted_iota(jnp.int32, (p.tokens, p.devices * ROWS), 0)
    col_in = lax.broadcasted_iota(jnp.int32, (p.tokens, p.devices * ROWS), 1)
    dest = row_in // p.quarter
    device = (row_in % p.quarter) // p.tok * PLANE + dest % 2 * 2 + dest // 2
    col_in = col_in - (device * ROWS + row_in % p.tok)
    flat = x[...].reshape(p.devices * ROWS, p.ext)
    for c in range(p.pieces):
        pick = jnp.where(col_in == c * p.tok, 1.0, 0.0).astype(BF16)
        got = jnp.dot(
            pick, flat if c == 0 else flat[:, : p.piece], preferred_element_type=F32
        )
        lhs[:, pl.ds(c * p.piece, p.piece)] = got[:, : p.piece].astype(BF16)
        if c == 0:
            lane = lax.broadcasted_iota(jnp.int32, (p.tokens, LANES), 1)
            terms = jnp.where(lane % SPLIT == e, got[:, p.piece :], 0.0)
            weight = jnp.sum(terms, axis=1, keepdims=True)
            table[...] = jnp.broadcast_to(weight, table.shape)

    @pl.loop(0, p.n_steps)
    def _(n):
        sums = [None, None]
        for m in range(p.per_n):
            first_copy(n, m).wait()
            k = m // 2
            part = jnp.dot(
                lhs[:, pl.ds(k * p.up_rows, p.up_rows)],
                wbuf[n * p.per_n + m, pl.ds(0, p.up_rows), pl.ds(0, p.up_cols)],
                preferred_element_type=F32,
            )
            sums[m % 2] = part if k == 0 else sums[m % 2] + part
        g, u = sums
        cols = pl.ds(pl.multiple_of(n * p.up_cols, p.up_cols), p.up_cols)
        hid[:, cols] = (g / (1.0 + jnp.exp(-g)) * u).astype(BF16)
        for m in range(p.per_n):
            @pl.when(n * p.per_n + m < p.downs)
            def _():
                down_copy(n * p.per_n + m).start()

    def copy_a(g):
        return remote(a_send.at[g], a_recv.at[g], sa.at[g], ra.at[g], core_peer)

    def copy_b(g):
        return remote(b_send.at[g], b_recv.at[g], sb.at[g], rb.at[g], y_peer)

    def copy_c(g, d):
        dest = lax.rem(slot + d, p.slots)
        return remote(
            z_send.at[g, dest], z_recv.at[g, d], sc.at[g, d], rc.at[g, d],
            dest * PLANE + e,
        )

    def compute(g):
        for i in range(p.group):
            j = g * p.group + i
            down_copy(j).wait()
            part = jnp.dot(
                hid[...], wbuf[j, pl.ds(0, p.hidden), pl.ds(0, p.down_cols)],
                preferred_element_type=F32,
            )
            part = part * table[:, 0:1]
            cols = pl.ds(i * p.down_cols, p.down_cols)
            low, high = part[: p.half], part[p.half :]
            is_low = core == 0
            keep[g, :, cols] = jnp.where(is_low, low, high)
            a_send[g, :, cols] = jnp.where(is_low, high, low).astype(BF16)
        copy_a(g).start()

    def second(g):
        copy_a(g).wait()
        total = keep[g] + a_recv[g].astype(F32)
        low, high = total[: p.quarter], total[p.quarter :]
        b_own[g] = jnp.where(ypos == 0, low, high)
        b_send[g] = jnp.where(ypos == 0, high, low).astype(BF16)
        copy_b(g).start()

    def third(g):
        copy_b(g).wait()
        z_full[...] = b_own[g] + b_recv[g].astype(F32)
        for s in range(p.slots):
            for c in range(p.pieces):
                z_stage[s, pl.ds(c * p.tok, p.tok), :] = z_full[
                    pl.ds(s * p.tok, p.tok), pl.ds(c * p.part, p.part)
                ]
        z_send[g] = z_stage[...].astype(BF16)
        b_own[g, pl.ds(0, ROWS), pl.ds(0, p.part)] = z_stage[slot]
        for d in range(1, p.slots):
            copy_c(g, d).start()

    @pl.loop(0, p.groups + 2 * LAG)
    def _(it):
        @pl.when(it < p.groups)
        def _():
            compute(it)

        @pl.when((it >= LAG) & (it < p.groups + LAG))
        def _():
            second(it - LAG)

        @pl.when(it >= 2 * LAG)
        def _():
            third(it - 2 * LAG)

    @pl.loop(0, p.groups)
    def _(g):
        total = b_own[g, pl.ds(0, ROWS), pl.ds(0, p.part)]
        for d in range(1, p.slots):
            copy_c(g, d).wait()
            total = total + z_recv[g, d].astype(F32)
        out_f32[...] = total
        for c in range(p.pieces):
            at = pl.multiple_of(g * p.cols + c * p.part, p.part)
            out_ref[:, pl.ds(at, p.part)] = out_f32[pl.ds(c * p.tok, p.tok), :].astype(BF16)

    for copy in started:
        copy.wait_send()


def shards(devices, tokens, expert_ids, router_weight, gate_weight, up_weight, down_weight):
    tok, width = tokens.shape
    experts = router_weight.shape[1]
    hidden = gate_weight.shape[2]
    p = Plan(devices, tok, width, hidden)
    vmem = pl.BlockSpec(memory_space=pltpu.VMEM)
    hbm = pl.BlockSpec(memory_space=pl.ANY)
    dma = pltpu.SemaphoreType.DMA
    scratch = [
        pltpu.VMEM((p.buffers, max(p.up_rows, hidden), max(p.up_cols, p.down_cols)), BF16),
        pltpu.VMEM((devices, ROWS, p.ext), BF16),
        pltpu.VMEM((ROWS, p.ext), F32),
        pltpu.VMEM((p.tokens, width), BF16),
        pltpu.VMEM((p.tokens, hidden), BF16),
        pltpu.VMEM((p.tokens, LANES), F32),
        pltpu.VMEM((p.groups, p.half, p.cols), F32),
        pltpu.VMEM((p.groups, p.half, p.cols), BF16),
        pltpu.VMEM((p.groups, p.half, p.cols), BF16),
        pltpu.VMEM((p.groups, p.quarter, p.cols), F32),
        pltpu.VMEM((p.groups, p.quarter, p.cols), BF16),
        pltpu.VMEM((p.groups, p.quarter, p.cols), BF16),
        pltpu.VMEM((p.quarter, p.cols), F32),
        pltpu.VMEM((p.slots, ROWS, p.part), F32),
        pltpu.VMEM((p.groups, p.slots, ROWS, p.part), BF16),
        pltpu.VMEM((p.groups, p.slots, ROWS, p.part), BF16),
        pltpu.VMEM((ROWS, p.part), F32),
        dma((p.buffers,)),
        dma((2, p.slots)), dma((2, p.slots)), dma((2, p.slots)), dma((2, p.slots)),
        dma((2, 2 * p.slots)), dma((2, 2 * p.slots)),
        dma((p.groups,)), dma((p.groups,)), dma((p.groups,)), dma((p.groups,)),
        dma((p.groups, p.slots)), dma((p.groups, p.slots)),
    ]
    return pl.pallas_call(
        functools.partial(kernel, p, experts),
        out_shape=jax.ShapeDtypeStruct((tok, width), BF16),
        in_specs=[vmem, pl.BlockSpec(memory_space=pltpu.SMEM), vmem, hbm, hbm, hbm],
        out_specs=vmem,
        scratch_shapes=scratch,
        compiler_params=pltpu.CompilerParams(
            collective_id=0, has_side_effects=True, vmem_limit_bytes=60 * 2**20
        ),
        cost_estimate=pl.CostEstimate(
            flops=6 * p.tokens * width * hidden,
            bytes_accessed=6 * width * hidden,
            transcendentals=p.tokens * hidden,
        ),
        name="moe_decode",
    )(tokens, expert_ids.T, router_weight.T, gate_weight, up_weight, down_weight)


def solution(mesh):
    return jax.shard_map(
        functools.partial(shards, mesh.shape["exp"]),
        mesh=mesh,
        in_specs=(
            P(("grp", "exp"), None),
            P(("grp", "exp"), None),
            P(),
            P("exp", None, None),
            P("exp", None, None),
            P("exp", None, None),
        ),
        out_specs=P(("grp", "exp"), None),
        check_vma=False,
    )
```

```python
import functools

import jax
import jax.numpy as jnp
from jax import lax
from jax.experimental import pallas as pl
from jax.experimental.pallas import tpu as pltpu
from jax.sharding import PartitionSpec as P

MESH = pl.DeviceIdType.MESH
F32 = jnp.float32
BF16 = jnp.bfloat16
LANES = 128
PLANE = 4
SPLIT = 32
LAG = 1
ROWS = 16


def divisor_at_most(total, most):
    return max(size for size in range(LANES, most + 1, LANES) if total % size == 0)


class Plan:
    def __init__(self, devices, tok, width, hidden):
        self.devices, self.tok, self.width, self.hidden = devices, tok, width, hidden
        self.slots = devices // PLANE
        self.pieces = ROWS // tok
        self.piece = width // self.pieces
        self.ext = self.piece + LANES
        middle = self.ext // LANES // 2 * LANES
        self.spans = ((0, middle), (middle, self.ext - middle))
        self.tokens = devices * tok
        self.half = self.tokens // 2
        self.quarter = self.tokens // 4
        self.up_rows = divisor_at_most(width, min(2048, 2 * hidden))
        self.up_cols = divisor_at_most(hidden, 512)
        self.k_steps = width // self.up_rows
        self.n_steps = hidden // self.up_cols
        self.per_n = 2 * self.k_steps
        self.first = self.per_n * self.n_steps
        self.down_cols = divisor_at_most(width, 512)
        self.downs = width // self.down_cols
        self.buffers = max(self.first, self.downs)
        self.group = 3
        self.groups = self.downs // self.group
        self.cols = self.group * self.down_cols
        self.part = self.cols // self.pieces


def kernel(
    p, experts, tok_ref, ids_ref, router_ref, gate_ref, up_ref, down_ref, out_ref,
    wbuf, x, stage, lhs, hid, table, keep, a_send, a_recv, b_own, b_send, b_recv,
    z_full, z_stage, z_send, z_recv, out_f32,
    wsem, gs_z, gr_z, gs_y, gr_y, gs_c, gr_c, sa, ra, sb, rb, sc, rc,
):
    grp = lax.axis_index("grp")
    me = lax.axis_index("exp")
    slot, e = me // PLANE, me % PLANE
    core, ypos = e % 2, e // 2
    core_peer = slot * PLANE + ypos * 2 + (1 - core)
    y_peer = slot * PLANE + (1 - ypos) * 2 + core

    def first_copy(n, m):
        k, ref = m // 2, (gate_ref, up_ref)[m % 2]
        at = n * p.per_n + m
        cols = pl.ds(pl.multiple_of(n * p.up_cols, p.up_cols), p.up_cols)
        return pltpu.make_async_copy(
            ref.at[0, pl.ds(k * p.up_rows, p.up_rows), cols],
            wbuf.at[at, pl.ds(0, p.up_rows), pl.ds(0, p.up_cols)],
            wsem.at[at],
        )

    def down_copy(j):
        cols = pl.ds(pl.multiple_of(j * p.down_cols, p.down_cols), p.down_cols)
        return pltpu.make_async_copy(
            down_ref.at[0, :, cols],
            wbuf.at[j, pl.ds(0, p.hidden), pl.ds(0, p.down_cols)],
            wsem.at[j],
        )

    def remote(src, dst, send, recv, device):
        return pltpu.make_async_remote_copy(
            src_ref=src, dst_ref=dst, send_sem=send, recv_sem=recv,
            device_id=(grp, device), device_id_type=MESH,
        )

    barrier = pltpu.get_barrier_semaphore()
    z_peers = [lax.rem(slot + d, p.slots) * PLANE + e for d in range(1, p.slots)]
    for peer in z_peers + [y_peer, core_peer]:
        pl.semaphore_signal(barrier, inc=1, device_id=(grp, peer), device_id_type=MESH)

    for m in range(p.per_n):
        first_copy(0, m).start()

    lane = lax.broadcasted_iota(jnp.int32, (p.tok, LANES), 1)
    line = lax.broadcasted_iota(jnp.int32, (p.tok, LANES), 0)
    id_a = jnp.zeros((p.tok, LANES), jnp.int32)
    id_b = id_a
    for t in range(p.tok):
        id_a = jnp.where(line == t, ids_ref[0, t], id_a)
        id_b = jnp.where(line == t, ids_ref[1, t], id_b)
    own = tok_ref[...].astype(F32)
    logit_a = jnp.zeros((p.tok, LANES), F32)
    logit_b = logit_a
    for expert in range(experts):
        row = router_ref[pl.ds(expert, 1), :].astype(F32)
        logit = jnp.sum(own * row, axis=1, keepdims=True)
        logit_a = jnp.where(id_a == expert, logit, logit_a)
        logit_b = jnp.where(id_b == expert, logit, logit_b)
    named = lane % SPLIT
    weight = jnp.where(named == id_a, 1.0 / (1.0 + jnp.exp(logit_b - logit_a)), 0.0)
    weight += jnp.where(named == id_b, 1.0 / (1.0 + jnp.exp(logit_a - logit_b)), 0.0)
    high = weight.astype(BF16).astype(F32)
    middle = (weight - high).astype(BF16).astype(F32)
    terms = jnp.where(lane < SPLIT, high, jnp.where(lane < 2 * SPLIT, middle, weight - high - middle))
    terms = jnp.where(lane < 3 * SPLIT, terms, 0.0)
    for c in range(p.pieces):
        rows = pl.ds(c * p.tok, p.tok)
        stage[rows, pl.ds(0, p.piece)] = tok_ref[:, pl.ds(c * p.piece, p.piece)].astype(F32)
        stage[rows, pl.ds(p.piece, LANES)] = terms
    x[me] = stage[...].astype(BF16)

    pl.semaphore_wait(barrier, p.slots + 1)

    started = []

    def send(copy):
        copy.start()
        started.append(copy)

    def block_copy(block, h, send_sems, recv_sems, at, device):
        cols = pl.ds(*p.spans[h])
        ref = x.at[block, :, cols]
        return remote(ref, ref, send_sems.at[h, at], recv_sems.at[h, at], device)

    def z_block(d):
        return lax.rem(slot + p.slots - d, p.slots) * PLANE

    spans = range(len(p.spans))
    for h in spans:
        for d in range(1, p.slots):
            send(block_copy(me, h, gs_z, gr_z, d, z_peers[d - 1]))
        send(block_copy(me, h, gs_y, gr_y, 0, y_peer))
    for h in spans:
        send(block_copy(me, h, gs_c, gr_c, 0, core_peer))

    for n in range(1, p.n_steps):
        for m in range(p.per_n):
            first_copy(n, m).start()
    for j in range(p.first, p.downs):
        down_copy(j).start()

    for h in spans:
        for d in range(1, p.slots):
            block = z_block(d) + e
            block_copy(block, h, gs_z, gr_z, d, core_peer).wait_recv()
            send(block_copy(block, h, gs_y, gr_y, d, y_peer))
            send(block_copy(block, h, gs_c, gr_c, d, core_peer))
    for h in spans:
        for d in range(p.slots):
            block = z_block(d) + (1 - ypos) * 2 + core
            block_copy(block, h, gs_y, gr_y, d, y_peer).wait_recv()
            send(block_copy(block, h, gs_c, gr_c, p.slots + d, core_peer))
    for h in spans:
        for side in range(2):
            ye = ypos if side == 0 else 1 - ypos
            for d in range(p.slots):
                block = z_block(d) + ye * 2 + (1 - core)
                at = side * p.slots + d
                block_copy(block, h, gs_c, gr_c, at, core_peer).wait_recv()

    row_in = lax.broadcasted_iota(jnp.int32, (p.tokens, p.devices * ROWS), 0)
    col_in = lax.broadcasted_iota(jnp.int32, (p.tokens, p.devices * ROWS), 1)
    dest = row_in // p.quarter
    device = (row_in % p.quarter) // p.tok * PLANE + dest % 2 * 2 + dest // 2
    col_in = col_in - (device * ROWS + row_in % p.tok)
    flat = x[...].reshape(p.devices * ROWS, p.ext)
    for c in range(p.pieces):
        pick = jnp.where(col_in == c * p.tok, 1.0, 0.0).astype(BF16)
        got = jnp.dot(
            pick, flat if c == 0 else flat[:, : p.piece], preferred_element_type=F32
        )
        lhs[:, pl.ds(c * p.piece, p.piece)] = got[:, : p.piece].astype(BF16)
        if c == 0:
            lane = lax.broadcasted_iota(jnp.int32, (p.tokens, LANES), 1)
            terms = jnp.where(lane % SPLIT == e, got[:, p.piece :], 0.0)
            weight = jnp.sum(terms, axis=1, keepdims=True)
            table[...] = jnp.broadcast_to(weight, table.shape)

    @pl.loop(0, p.n_steps)
    def _(n):
        sums = [None, None]
        for m in range(p.per_n):
            first_copy(n, m).wait()
            k = m // 2
            part = jnp.dot(
                lhs[:, pl.ds(k * p.up_rows, p.up_rows)],
                wbuf[n * p.per_n + m, pl.ds(0, p.up_rows), pl.ds(0, p.up_cols)],
                preferred_element_type=F32,
            )
            sums[m % 2] = part if k == 0 else sums[m % 2] + part
        g, u = sums
        cols = pl.ds(pl.multiple_of(n * p.up_cols, p.up_cols), p.up_cols)
        hid[:, cols] = (g / (1.0 + jnp.exp(-g)) * u).astype(BF16)
        for m in range(p.per_n):
            @pl.when(n * p.per_n + m < p.downs)
            def _():
                down_copy(n * p.per_n + m).start()

    def copy_a(g):
        return remote(a_send.at[g], a_recv.at[g], sa.at[g], ra.at[g], core_peer)

    def copy_b(g):
        return remote(b_send.at[g], b_recv.at[g], sb.at[g], rb.at[g], y_peer)

    def copy_c(g, d):
        dest = lax.rem(slot + d, p.slots)
        return remote(
            z_send.at[g, dest], z_recv.at[g, d], sc.at[g, d], rc.at[g, d],
            dest * PLANE + e,
        )

    def compute(g):
        for i in range(p.group):
            j = g * p.group + i
            down_copy(j).wait()
            part = jnp.dot(
                hid[...], wbuf[j, pl.ds(0, p.hidden), pl.ds(0, p.down_cols)],
                preferred_element_type=F32,
            )
            part = part * table[:, 0:1]
            cols = pl.ds(i * p.down_cols, p.down_cols)
            low, high = part[: p.half], part[p.half :]
            is_low = core == 0
            keep[g, :, cols] = jnp.where(is_low, low, high)
            a_send[g, :, cols] = jnp.where(is_low, high, low).astype(BF16)
        copy_a(g).start()

    def second(g):
        copy_a(g).wait()
        total = keep[g] + a_recv[g].astype(F32)
        low, high = total[: p.quarter], total[p.quarter :]
        b_own[g] = jnp.where(ypos == 0, low, high)
        b_send[g] = jnp.where(ypos == 0, high, low).astype(BF16)
        copy_b(g).start()

    def third(g):
        copy_b(g).wait()
        z_full[...] = b_own[g] + b_recv[g].astype(F32)
        for s in range(p.slots):
            for c in range(p.pieces):
                z_stage[s, pl.ds(c * p.tok, p.tok), :] = z_full[
                    pl.ds(s * p.tok, p.tok), pl.ds(c * p.part, p.part)
                ]
        z_send[g] = z_stage[...].astype(BF16)
        b_own[g, pl.ds(0, ROWS), pl.ds(0, p.part)] = z_stage[slot]
        for d in range(1, p.slots):
            copy_c(g, d).start()

    @pl.loop(0, p.groups + 2 * LAG)
    def _(it):
        @pl.when(it < p.groups)
        def _():
            compute(it)

        @pl.when((it >= LAG) & (it < p.groups + LAG))
        def _():
            second(it - LAG)

        @pl.when(it >= 2 * LAG)
        def _():
            third(it - 2 * LAG)

    @pl.loop(0, p.groups)
    def _(g):
        total = b_own[g, pl.ds(0, ROWS), pl.ds(0, p.part)]
        for d in range(1, p.slots):
            copy_c(g, d).wait()
            total = total + z_recv[g, d].astype(F32)
        out_f32[...] = total
        for c in range(p.pieces):
            at = pl.multiple_of(g * p.cols + c * p.part, p.part)
            out_ref[:, pl.ds(at, p.part)] = out_f32[pl.ds(c * p.tok, p.tok), :].astype(BF16)

    for copy in started:
        copy.wait_send()


def shards(devices, tokens, expert_ids, router_weight, gate_weight, up_weight, down_weight):
    tok, width = tokens.shape
    experts = router_weight.shape[1]
    hidden = gate_weight.shape[2]
    p = Plan(devices, tok, width, hidden)
    vmem = pl.BlockSpec(memory_space=pltpu.VMEM)
    hbm = pl.BlockSpec(memory_space=pl.ANY)
    dma = pltpu.SemaphoreType.DMA
    scratch = [
        pltpu.VMEM((p.buffers, max(p.up_rows, hidden), max(p.up_cols, p.down_cols)), BF16),
        pltpu.VMEM((devices, ROWS, p.ext), BF16),
        pltpu.VMEM((ROWS, p.ext), F32),
        pltpu.VMEM((p.tokens, width), BF16),
        pltpu.VMEM((p.tokens, hidden), BF16),
        pltpu.VMEM((p.tokens, LANES), F32),
        pltpu.VMEM((p.groups, p.half, p.cols), F32),
        pltpu.VMEM((p.groups, p.half, p.cols), BF16),
        pltpu.VMEM((p.groups, p.half, p.cols), BF16),
        pltpu.VMEM((p.groups, p.quarter, p.cols), F32),
        pltpu.VMEM((p.groups, p.quarter, p.cols), BF16),
        pltpu.VMEM((p.groups, p.quarter, p.cols), BF16),
        pltpu.VMEM((p.quarter, p.cols), F32),
        pltpu.VMEM((p.slots, ROWS, p.part), F32),
        pltpu.VMEM((p.groups, p.slots, ROWS, p.part), BF16),
        pltpu.VMEM((p.groups, p.slots, ROWS, p.part), BF16),
        pltpu.VMEM((ROWS, p.part), F32),
        dma((p.buffers,)),
        dma((2, p.slots)), dma((2, p.slots)), dma((2, p.slots)), dma((2, p.slots)),
        dma((2, 2 * p.slots)), dma((2, 2 * p.slots)),
        dma((p.groups,)), dma((p.groups,)), dma((p.groups,)), dma((p.groups,)),
        dma((p.groups, p.slots)), dma((p.groups, p.slots)),
    ]
    return pl.pallas_call(
        functools.partial(kernel, p, experts),
        out_shape=jax.ShapeDtypeStruct((tok, width), BF16),
        in_specs=[vmem, pl.BlockSpec(memory_space=pltpu.SMEM), vmem, hbm, hbm, hbm],
        out_specs=vmem,
        scratch_shapes=scratch,
        compiler_params=pltpu.CompilerParams(
            collective_id=0, has_side_effects=True, vmem_limit_bytes=60 * 2**20
        ),
        cost_estimate=pl.CostEstimate(
            flops=6 * p.tokens * width * hidden,
            bytes_accessed=6 * width * hidden,
            transcendentals=p.tokens * hidden,
        ),
        name="moe_decode",
    )(tokens, expert_ids.T, router_weight.T, gate_weight, up_weight, down_weight)


def solution(mesh):
    return jax.shard_map(
        functools.partial(shards, mesh.shape["exp"]),
        mesh=mesh,
        in_specs=(
            P(("grp", "exp"), None),
            P(("grp", "exp"), None),
            P(),
            P("exp", None, None),
            P("exp", None, None),
            P("exp", None, None),
        ),
        out_specs=P(("grp", "exp"), None),
        check_vma=False,
    )
```
